32 devices in a mesh: dp: 4 (over y, x), seq: 2 (over core), tensor: 4 (over z).
Axes of the slice: x: 2, y: 2, z: 4, core: 2. Of those that a mesh axis runs over, the one named last changes fastest.
Arguments:
- tokens: bfloat16 [4096, 8192], P(('dp', 'seq'), 'tensor'), may hold values from -6 to 6
- out_grad: bfloat16 [4096, 8192], P(('dp', 'seq'), 'tensor'), may hold values from -6 to 6
- up_perm: int32 [2, 8, 8], replicated, may hold values from 0 to 7, each once within a row
- down_perm: int32 [2, 8, 8], replicated, may hold values from 0 to 7, each once within a row
- up_weight: bfloat16 [64, 2, 256, 256], P('tensor'), may hold values from -0.25 to 0.25
- down_weight: bfloat16 [64, 2, 256, 256], P('tensor'), may hold values from -0.1875 to 0.1875
Outputs:
- output: bfloat16 [4096, 8192], P(('dp', 'seq'), 'tensor')
- input_grad: bfloat16 [4096, 8192], P(('dp', 'seq'), 'tensor')
- grad_up: float32 [64, 2, 256, 256], P('tensor', None, ('dp', 'seq'))
- grad_down: float32 [64, 2, 256, 256], P('tensor', None, ('dp', 'seq'))
The draws below stay inside these ranges and needn't reach their ends.
Inputs may be any that keep to these rules, and one draw needn't show every extreme that they name: `up_perm`: for each section, every run of 8 consecutive entries along the last dimension is a permutation of 0 to 7. `down_perm`: for each section, every run of 8 consecutive entries along the last dimension is a permutation of 0 to 7.
All inputs are finite; a program needn't handle non-finite values.
Results may differ from the reference program's by a relative error of at most 0.0049.
Values may be sent and summed in bfloat16 or wider, within the bound.
No kernel may reach another device: no remote copies, remote signals or barrier semaphores. Data moves between devices by JAX's collectives and lax.ppermute only.
A program may use at most 128 MiB of HBM per device.

```python
import jax
import jax.numpy as jnp
from jax import lax

D = 8192
FF = 16384
B = 256
SECTIONS = 2
NB = 32
HB = 64
GROUPS = 4
FPD = 8
HPD = 16
TOKENS = 4096


def block_levels(rng, extent, cuts, least, top_value):
    gain, own = 1.0, jax.random.fold_in(rng, 6)
    for position, blocks in cuts:
        steps = jnp.exp(jax.random.uniform(jax.random.fold_in(own, position), (blocks,), jnp.float32, least / len(cuts), top_value / len(cuts)))
        gain = gain * jnp.repeat(steps, extent[position] // blocks).reshape([-1 if axis == position else 1 for axis in range(len(extent))])
    return gain


def centred(rng, shape, width, limit, shards=(), kind=jnp.bfloat16):
    result = jax.random.normal(rng, shape, jnp.float32) * width
    if len(shards) > 0:
        result = block_levels(rng, shape, shards, -0.22, 0.18) * result
    return jnp.clip(result, min=-limit, max=limit).astype(kind)


def setup_inputs(seed: int = 0) -> dict:
    key_of = jax.random.split(jax.random.key(seed), 7)
    tokens = centred(key_of[0], (TOKENS, D), 1.0, 6.0, ((0, 8), (1, 4)))
    out_grad = centred(key_of[1], (TOKENS, D), 1.0, 6.0, ((0, 8), (1, 4)))
    up_perm = jax.vmap(lambda own: jax.random.permutation(own, FPD))(jax.random.split(key_of[2], SECTIONS * (HB // FPD))).reshape((SECTIONS, HB // FPD, FPD)).astype(jnp.int32)
    down_perm = jax.vmap(lambda own: jax.random.permutation(own, FPD))(jax.random.split(key_of[3], SECTIONS * (HB // FPD))).reshape((SECTIONS, HB // FPD, FPD)).astype(jnp.int32)
    up_weight = centred(key_of[4], (HB, SECTIONS, B, B), (SECTIONS * B) ** -0.5, 0.25, ((0, 4),))
    down_weight = centred(key_of[5], (HB, SECTIONS, B, B), (2 * FF // NB) ** -0.5, 0.1875, ((0, 4),))
    return {"tokens": tokens, "out_grad": out_grad, "up_perm": up_perm, "down_perm": down_perm, "up_weight": up_weight, "down_weight": down_weight}


def block_index(perm_flat, hidx, section_id):
    group_id = hidx // HPD
    paired = (group_id + section_id * (GROUPS // 2)) % GROUPS
    return (paired * FPD + perm_flat[section_id, hidx]).astype(jnp.int32)

def add_block(accum, term, block_id):
    start = (block_id * B).astype(jnp.int32)
    current = lax.dynamic_slice_in_dim(accum, start, B, 1)
    return lax.dynamic_update_slice_in_dim(accum, current + term, start, 1)

def reference(tokens, out_grad, up_perm, down_perm, up_weight, down_weight):
    grad_scale = float(TOKENS) ** (-0.5)
    up_flat = up_perm.reshape(SECTIONS, HB)
    down_flat = down_perm.reshape(SECTIONS, HB)

    def one_block(carry, inputs):
        out_acc, back_acc = carry
        hidx, up_blk, down_blk = inputs
        in_ids = [block_index(up_flat, hidx, 0), block_index(up_flat, hidx, 1)]
        out_ids = [block_index(down_flat, hidx, 0), block_index(down_flat, hidx, 1)]
        in_cols = [lax.dynamic_slice_in_dim(tokens, (blk * B).astype(jnp.int32), B, 1) for blk in in_ids]
        grad_cols = [lax.dynamic_slice_in_dim(out_grad, (blk * B).astype(jnp.int32), B, 1) for blk in out_ids]
        pre_act = jnp.dot(in_cols[0], up_blk[0], preferred_element_type=jnp.float32)
        pre_act = pre_act + jnp.dot(in_cols[1], up_blk[1], preferred_element_type=jnp.float32)
        hidden = jax.nn.gelu(pre_act).astype(jnp.bfloat16)
        out_acc = add_block(out_acc, jnp.dot(hidden, down_blk[0], preferred_element_type=jnp.float32), out_ids[0])
        out_acc = add_block(out_acc, jnp.dot(hidden, down_blk[1], preferred_element_type=jnp.float32), out_ids[1])
        d_hidden = jnp.dot(grad_cols[0], down_blk[0].T, preferred_element_type=jnp.float32)
        d_hidden = d_hidden + jnp.dot(grad_cols[1], down_blk[1].T, preferred_element_type=jnp.float32)
        _, pull_back = jax.vjp(jax.nn.gelu, pre_act)
        d_pre = pull_back(d_hidden)[0].astype(jnp.bfloat16)
        grad_dn = jnp.stack([jnp.dot(hidden.T, grad_cols[0], preferred_element_type=jnp.float32), jnp.dot(hidden.T, grad_cols[1], preferred_element_type=jnp.float32)]) * grad_scale
        grad_upb = jnp.stack([jnp.dot(in_cols[0].T, d_pre, preferred_element_type=jnp.float32), jnp.dot(in_cols[1].T, d_pre, preferred_element_type=jnp.float32)]) * grad_scale
        back_acc = add_block(back_acc, jnp.dot(d_pre, up_blk[0].T, preferred_element_type=jnp.float32), in_ids[0])
        back_acc = add_block(back_acc, jnp.dot(d_pre, up_blk[1].T, preferred_element_type=jnp.float32), in_ids[1])
        return ((out_acc, back_acc), (grad_upb, grad_dn))
    zeros_out = jnp.zeros((TOKENS, D), jnp.float32)
    zeros_back = jnp.zeros((TOKENS, D), jnp.float32)
    hidx_all = jnp.arange(HB, dtype=jnp.int32)
    (out_acc, back_acc), (grad_up, grad_down) = lax.scan(one_block, (zeros_out, zeros_back), (hidx_all, up_weight, down_weight))
    return (out_acc.astype(jnp.bfloat16), back_acc.astype(jnp.bfloat16), grad_up, grad_down)
```

```python
import functools
import math

import jax
import jax.numpy as jnp
from jax import lax
from jax.experimental import pallas as pl
from jax.experimental.pallas import tpu as pltpu
from jax.sharding import PartitionSpec as P

F32 = jnp.float32
BF16 = jnp.bfloat16
ROOT = math.sqrt(2.0 / math.pi)
CUBIC = 0.044715


def dot(a, b, over):
    return lax.dot_general(a, b, ((over[:1], over[1:]), ((), ())), preferred_element_type=F32)


def activate(pre, d_hidden):
    square = pre * pre
    tanh = jnp.tanh(ROOT * (pre + CUBIC * (square * pre)))
    cdf = 0.5 * (1.0 + tanh)
    slope = cdf + (0.5 * ROOT) * pre * (1.0 - tanh * tanh) * (1.0 + (3.0 * CUBIC) * square)
    return (pre * cdf).astype(BF16), (d_hidden * slope).astype(BF16)


def layer_kernel(first, rows, ids, *refs):
    refs = list(refs)
    take = lambda count: [refs.pop(0) for _ in range(count)]
    chunks = 1 if first else 2
    (x_near,), x_far = take(1), take(chunks)
    (g_near,), g_far = take(1), take(chunks)
    up, down = take(2)
    if not first:
        hidden_before, d_pre_before = take(2)
    result = take(4)
    if first:
        hidden_out, d_pre_out = take(2)
    else:
        sums = take(8)
    xs, gs, out_acc, back_acc = take(4)
    if not first:
        up_sum, down_sum = take(2)
    step = pl.program_id(0)
    steps = pl.num_programs(0)
    blocks, _, size = xs.shape
    half = blocks // 2
    low = 0 if first else rows[0]
    count = rows[0] if first else rows[1]

    @pl.when(step == 0)
    def _():
        for dst, near, far in ((xs, x_near, x_far), (gs, g_near, g_far)):
            for b in range(half):
                cols = slice(b * size, (b + 1) * size)
                dst[b] = near[:, cols]
                at = 0
                for part in far:
                    dst[half + b, at : at + part.shape[0]] = part[:, cols]
                    at += part.shape[0]
        out_acc[...] = jnp.zeros_like(out_acc)
        back_acc[...] = jnp.zeros_like(back_acc)

    in0, in1, out0, out1 = (ids[k, step] for k in range(4))
    now = pl.ds(low, count)
    x_cat = jnp.concatenate([xs[in0, now], xs[in1, now]], axis=1)
    g_cat = jnp.concatenate([gs[out0, now], gs[out1, now]], axis=1)
    up_cat = up[0].reshape(2 * size, size)
    down_cat = jnp.concatenate([down[0, 0], down[0, 1]], axis=1)
    pre = dot(x_cat, up_cat, (1, 0))
    d_hidden = dot(g_cat, down_cat, (1, 1))
    hidden, d_pre = activate(pre, d_hidden)
    out = dot(hidden, down_cat, (1, 0))
    back = dot(d_pre, up_cat, (1, 1))
    out_acc[out0] += out[:, :size]
    out_acc[out1] += out[:, size:]
    back_acc[in0] += back[:, :size]
    back_acc[in1] += back[:, size:]
    if first:
        hidden_out[0] = hidden
        d_pre_out[0] = d_pre
    else:
        before = pl.ds(0, low)
        x_before = jnp.concatenate([xs[in0, before], xs[in1, before]], axis=1)
        g_before = jnp.concatenate([gs[out0, before], gs[out1, before]], axis=1)
        up_sum[...] = dot(x_cat, d_pre, (0, 0)) + dot(x_before, d_pre_before[0], (0, 0))
        down_sum[...] = dot(hidden, g_cat, (0, 0)) + dot(hidden_before[0], g_before, (0, 0))
        me = ids[4, 0]
        shard = sums[0].shape[3]
        shards = size // shard

        def store(keep_up, send_up, keep_down, send_down):
            for place in range(shards):
                start = pl.multiple_of((place ^ me) * shard, shard)
                to_up, to_down = (send_up, send_down) if place & 1 else (keep_up, keep_down)
                for s in range(2):
                    to_up[place >> 1, 0, s] = up_sum[pl.ds(s * size + start, shard)].astype(BF16)
                    to_down[place >> 1, 0, s] = down_sum[
                        pl.ds(start, shard), s * size : (s + 1) * size
                    ].astype(BF16)

        pl.when(step < steps // 2)(lambda: store(*sums[:4]))
        pl.when(step >= steps // 2)(lambda: store(*sums[4:]))

    @pl.when(step == steps - 1)
    def _():
        for b in range(blocks):
            side, cols = divmod(b, half)
            cols = slice(cols * size, (cols + 1) * size)
            result[side][:, cols] = out_acc[b].astype(BF16)
            result[2 + side][:, cols] = back_acc[b].astype(BF16)


def layer(first, rows, shards, ids, x_near, x_far, g_near, g_far, up, down, before=()):
    steps, _, size, _ = up.shape
    width = x_near.shape[1]
    blocks = 2 * width // size
    hid = steps // 2
    all_rows = rows[0] if first else sum(rows)
    count = rows[0] if first else rows[1]

    def whole(shape):
        return pl.BlockSpec(shape, lambda i, ids: (0,) * len(shape))

    weight = pl.BlockSpec((1, 2, size, size), lambda i, ids: (i, 0, 0, 0))
    kept = pl.BlockSpec((1, rows[0], size), lambda i, ids: (i, 0, 0))
    far = [whole(part.shape) for part in x_far]
    near = whole((all_rows, width))
    in_specs = [near, *far, near, *far, weight, weight]
    out_shape = [jax.ShapeDtypeStruct((count, width), BF16)] * 4
    out_specs = [whole((count, width))] * 4
    scratch = [
        pltpu.VMEM((blocks, all_rows, size), BF16),
        pltpu.VMEM((blocks, all_rows, size), BF16),
        pltpu.VMEM((blocks, count, size), F32),
        pltpu.VMEM((blocks, count, size), F32),
    ]
    if first:
        out_shape += [jax.ShapeDtypeStruct((steps, count, size), BF16)] * 2
        out_specs += [kept] * 2
    else:
        in_specs += [kept] * 2
        shard = size // shards
        out_shape += [jax.ShapeDtypeStruct((shards // 2, hid, 2, shard, size), BF16)] * 8
        for part in range(2):
            out_specs += [
                pl.BlockSpec(
                    (shards // 2, 1, 2, shard, size),
                    lambda i, ids, part=part: (0, jnp.clip(i - part * hid, 0, hid - 1), 0, 0, 0),
                )
            ] * 4
        scratch += [pltpu.VMEM((2 * size, size), F32), pltpu.VMEM((size, 2 * size), F32)]
    flops = steps * size * size * 2 * (8 * count + (0 if first else 4 * all_rows))
    return pl.pallas_call(
        functools.partial(layer_kernel, first, rows),
        out_shape=out_shape,
        grid_spec=pltpu.PrefetchScalarGridSpec(
            num_scalar_prefetch=1,
            grid=(steps,),
            in_specs=in_specs,
            out_specs=out_specs,
            scratch_shapes=scratch,
        ),
        compiler_params=pltpu.CompilerParams(
            dimension_semantics=("arbitrary",), vmem_limit_bytes=60 << 20
        ),
        cost_estimate=pl.CostEstimate(flops=flops, bytes_accessed=40 << 20, transcendentals=0),
    )(ids, x_near, *x_far, g_near, *g_far, up, down, *before)


def hop(block, bit):
    seq = lax.axis_size("seq")
    axis, bit = ("seq", bit) if bit < seq else ("dp", bit // seq)
    return lax.ppermute(block, axis, [(i, i ^ bit) for i in range(lax.axis_size(axis))])


def plane_bits():
    seq, dp = lax.axis_size("seq"), lax.axis_size("dp")
    return (
        [1 << k for k in range(seq.bit_length() - 1)],
        [seq << k for k in range(dp.bit_length() - 1)],
    )


def gather(shard, order):
    parts = {0: shard}
    for bit in order:
        for place in list(parts):
            parts[place | bit] = hop(parts[place], bit)
    return parts


def total(terms):
    return sum(term.astype(F32) for term in terms)


def reduce_scatter(keep, send, order):
    count = keep.shape[0]
    got = hop(send, order[0])
    terms = {2 * p: [keep[p], got[p]] for p in range(count)}
    for bit in order[1:]:
        away = [p for p in terms if p & bit]
        got = hop(jnp.stack([total(terms[p]).astype(BF16) for p in away]), bit)
        for k, p in enumerate(away):
            terms[p ^ bit].append(got[k])
            del terms[p]
    return total(terms[0])


def on_device(tokens, out_grad, up_perm, down_perm, up_weight, down_weight):
    tok_rows, width = tokens.shape
    hid, _, size, _ = up_weight.shape
    groups, group = lax.axis_size("tensor"), lax.axis_index("tensor")
    blocks = width // size
    away = groups // 2
    seq_bits, dp_bits = plane_bits()
    shards = lax.axis_size("dp") * lax.axis_size("seq")
    me = lax.axis_index("dp") * lax.axis_size("seq") + lax.axis_index("seq")
    pairs = [(p, p + away) if p % 2 == 0 else (p + away, p) for p in range(away)]
    into = [(other, worker) for worker, other in pairs]
    back = pairs
    works = (group % away % 2 == 0) != (group >= away)
    partner = (group + away) % groups

    rows = (tok_rows // 2, tok_rows - tok_rows // 2)
    lines = hid * 2 * size // shards

    def weight_shard(weight):
        return lax.dynamic_slice_in_dim(weight.reshape(-1, size), me * lines, lines, 0)

    up_shard = lax.ppermute(weight_shard(up_weight), "tensor", into)
    down_shard = lax.ppermute(weight_shard(down_weight), "tensor", into)
    x_far, g_far = [], []
    for low, high in ((0, rows[0]), (rows[0], tok_rows)):
        x_far.append(lax.ppermute(tokens[low:high], "tensor", into))
        g_far.append(lax.ppermute(out_grad[low:high], "tensor", into))

    def both(weight, parts):
        table = jnp.concatenate(
            [jnp.zeros((shards, lines, size), BF16), weight.reshape(shards, lines, size)]
        )
        for place, part in parts.items():
            table = lax.dynamic_update_slice_in_dim(table, part[None], place ^ me, 0)
        return table.reshape(2 * hid, 2, size, size)

    up = both(up_weight, gather(up_shard, dp_bits + seq_bits))
    down = both(down_weight, gather(down_shard, dp_bits[::-1] + seq_bits))

    def block_ids(perm):
        flat = perm.reshape(2, -1)
        theirs = lax.dynamic_slice_in_dim(flat, partner * hid, hid, 1)
        mine = lax.dynamic_slice_in_dim(flat, group * hid, hid, 1)
        side = jnp.array([[0], [blocks]], jnp.int32)
        return jnp.concatenate([theirs + side[::-1], mine + side], axis=1)

    ids = jnp.concatenate(
        [
            block_ids(up_perm),
            block_ids(down_perm),
            jnp.full((1, 2 * hid), me, jnp.int32),
        ]
    )

    one = layer(True, rows, shards, ids, tokens, x_far[:1], out_grad, g_far[:1], up, down)
    two = layer(False, rows, shards, ids, tokens, x_far, out_grad, g_far, up, down, one[4:6])

    def deliver(near, far):
        got = [lax.ppermute(part, "tensor", back) for part in far]
        return jnp.concatenate([jnp.where(works, n, f) for n, f in zip(near, got)])

    output = deliver((one[0], two[0]), (one[1], two[1]))
    input_grad = deliver((one[2], two[2]), (one[3], two[3]))

    orders = (seq_bits + dp_bits, seq_bits + dp_bits[::-1])
    sums = two[4:]
    theirs = [
        lax.ppermute(
            reduce_scatter(sums[2 * k], sums[2 * k + 1], orders[k]).astype(BF16), "tensor", back
        )
        for k in range(2)
    ]
    mine = [reduce_scatter(sums[4 + 2 * k], sums[5 + 2 * k], orders[k]) for k in range(2)]
    scale = float(tok_rows * shards) ** (-0.5)
    grads = [jnp.where(works, m, t.astype(F32)) * scale for m, t in zip(mine, theirs)]
    return output, input_grad, grads[0], grads[1]


def solution(mesh):
    in_specs = (
        P(("dp", "seq"), "tensor"),
        P(("dp", "seq"), "tensor"),
        P(),
        P(),
        P("tensor", None, None, None),
        P("tensor", None, None, None),
    )
    out_specs = (
        P(("dp", "seq"), "tensor"),
        P(("dp", "seq"), "tensor"),
        P("tensor", None, ("dp", "seq"), None),
        P("tensor", None, ("dp", "seq"), None),
    )
    return jax.shard_map(
        on_device, mesh=mesh, in_specs=in_specs, out_specs=out_specs, check_vma=False
    )
```

```python
import functools
import math

import jax
import jax.numpy as jnp
from jax import lax
from jax.experimental import pallas as pl
from jax.experimental.pallas import tpu as pltpu
from jax.sharding import PartitionSpec as P

F32 = jnp.float32
BF16 = jnp.bfloat16
ROOT = math.sqrt(2.0 / math.pi)
CUBIC = 0.044715


def dot(a, b, over):
    return lax.dot_general(a, b, ((over[:1], over[1:]), ((), ())), preferred_element_type=F32)


def activate(pre, d_hidden):
    square = pre * pre
    tanh = jnp.tanh(pre * (ROOT + (ROOT * CUBIC) * square))
    cdf = 0.5 + 0.5 * tanh
    slope = cdf + pre * (0.5 - 0.5 * tanh * tanh) * (ROOT + (3.0 * ROOT * CUBIC) * square)
    return (pre * cdf).astype(BF16), (d_hidden * slope).astype(BF16)


def layer_kernel(first, rows, slots, ids, *refs):
    refs = list(refs)
    take = lambda count: [refs.pop(0) for _ in range(count)]
    near = take(2)
    far = take(1 if first else 2)
    up_far, down_far, up_near, down_near = take(4)
    if not first:
        hidden_before, d_pre_before = take(2)
    near_out = take(2)
    (far_out,) = take(1)
    if first:
        hidden_out, d_pre_out = take(2)
    else:
        sums = take(4)
    out_acc, back_acc = take(2)
    if not first:
        up_sum, down_sum = take(2)
    step = pl.program_id(0)
    steps = pl.num_programs(0)
    each, _, size, _ = up_far.shape
    low = 0 if first else rows[0]
    count = rows[0] if first else rows[1]

    @pl.when(step == 0)
    def _():
        out_acc[...] = jnp.zeros_like(out_acc)
        back_acc[...] = jnp.zeros_like(back_acc)

    theirs = step < steps // 2

    def columns(block):
        return pl.ds(pl.multiple_of(block * size, size), size)

    def both(k, at, part):
        chunk = pl.ds(0, rows[0]) if part == 0 else pl.ds(rows[0], rows[1])
        return jnp.concatenate([near[k][chunk, at[0]], far[part][k, :, at[1]]], axis=1)

    def pick(theirs_ref, ours_ref, e):
        return [jnp.where(theirs, theirs_ref[e, 1 - s], ours_ref[e, s]) for s in range(2)]

    work = []
    for e in range(each):
        ins = [columns(ids[k, step * each + e]) for k in (0, 1)]
        outs = [columns(ids[k, step * each + e]) for k in (2, 3)]
        up_cat = jnp.concatenate(pick(up_far, up_near, e), axis=0)
        down_cat = jnp.concatenate(pick(down_far, down_near, e), axis=1)
        part = 0 if first else 1
        x_cat = both(0, ins, part)
        g_cat = both(1, outs, part)
        pre = dot(x_cat, up_cat, (1, 0))
        d_hidden = dot(g_cat, down_cat, (1, 1))
        work.append((ins, outs, x_cat, g_cat, up_cat, down_cat, pre, d_hidden))
    done = []
    for e, (ins, outs, x_cat, g_cat, up_cat, down_cat, pre, d_hidden) in enumerate(work):
        hidden, d_pre = activate(pre, d_hidden)
        done.append((dot(hidden, down_cat, (1, 0)), dot(d_pre, up_cat, (1, 1))))
        if first:
            hidden_out[e] = hidden
            d_pre_out[e] = d_pre
        else:
            up_sum[e] = dot(x_cat, d_pre, (0, 0)) + dot(both(0, ins, 0), d_pre_before[e], (0, 0))
            down_sum[e] = dot(hidden, g_cat, (0, 0)) + dot(hidden_before[e], both(1, outs, 0), (0, 0))
    for (ins, outs, *_), (out, back) in zip(work, done):
        for s in range(2):
            out_acc[s, :, outs[s]] += out[:, s * size : (s + 1) * size]
            back_acc[s, :, ins[s]] += back[:, s * size : (s + 1) * size]
    if not first:
        me = ids[4, 0]
        shard = sums[0].shape[4]
        shards = size // shard

        def store(keep, send, flip):
            for e in range(each):
                for place in range(shards):
                    start = pl.multiple_of((place ^ me) * shard, shard)
                    to = send if place & 1 else keep
                    for s in range(2):
                        at = (1 - s if flip else s) * size
                        to[0, slots[0][place], e, s] = up_sum[
                            e, pl.ds(at + start, shard)
                        ].astype(BF16)
                        to[1, slots[1][place], e, s] = down_sum[
                            e, pl.ds(start, shard), at : at + size
                        ].astype(BF16)

        pl.when(theirs)(lambda: store(*sums[:2], True))
        pl.when(jnp.logical_not(theirs))(lambda: store(*sums[2:], False))

    @pl.when(step == steps - 1)
    def _():
        for k, acc in enumerate((out_acc, back_acc)):
            near_out[k][...] = acc[0].astype(BF16)
            far_out[k] = acc[1].astype(BF16)


def layer(first, rows, slots, each, ids, near, far, up_far, down_far, up, down, before=()):
    hid, _, size, _ = up.shape
    width = near[0].shape[1]
    shards = len(slots[0])
    all_rows = rows[0] if first else sum(rows)
    count = rows[0] if first else rows[1]
    turns = hid // each
    steps = 2 * turns

    def whole(shape):
        return pl.BlockSpec(shape, lambda i, ids: (0,) * len(shape))

    def weight(part):
        return pl.BlockSpec(
            (each, 2, size, size),
            lambda i, ids: (jnp.clip(i - part * turns, 0, turns - 1), 0, 0, 0),
        )

    kept = pl.BlockSpec((each, rows[0], size), lambda i, ids: (i, 0, 0))
    in_specs = [whole((all_rows, width))] * 2 + [whole(part.shape) for part in far]
    in_specs += [weight(0)] * 2 + [weight(1)] * 2
    out_shape = [jax.ShapeDtypeStruct((count, width), BF16)] * 2
    out_shape += [jax.ShapeDtypeStruct((2, count, width), BF16)]
    out_specs = [whole(out.shape) for out in out_shape]
    scratch = [pltpu.VMEM((2, count, width), F32)] * 2
    if first:
        out_shape += [jax.ShapeDtypeStruct((2 * hid, count, size), BF16)] * 2
        out_specs += [kept] * 2
    else:
        in_specs += [kept] * 2
        shard = size // shards
        out_shape += [jax.ShapeDtypeStruct((2, shards // 2, hid, 2, shard, size), BF16)] * 4
        for part in range(2):
            out_specs += [
                pl.BlockSpec(
                    (2, shards // 2, each, 2, shard, size),
                    lambda i, ids, part=part: (
                        *(0, 0, jnp.clip(i - part * turns, 0, turns - 1)),
                        *(0, 0, 0),
                    ),
                )
            ] * 2
        scratch += [
            pltpu.VMEM((each, 2 * size, size), F32),
            pltpu.VMEM((each, size, 2 * size), F32),
        ]
    return pl.pallas_call(
        functools.partial(layer_kernel, first, rows, slots),
        out_shape=out_shape,
        grid_spec=pltpu.PrefetchScalarGridSpec(
            num_scalar_prefetch=1,
            grid=(steps,),
            in_specs=in_specs,
            out_specs=out_specs,
            scratch_shapes=scratch,
        ),
        compiler_params=pltpu.CompilerParams(
            dimension_semantics=("arbitrary",), vmem_limit_bytes=60 << 20
        ),
        cost_estimate=pl.CostEstimate(flops=0, bytes_accessed=0, transcendentals=0),
    )(ids, *near, *far, up_far, down_far, up, down, *before)


def hop(block, bit):
    seq = lax.axis_size("seq")
    axis, bit = ("seq", bit) if bit < seq else ("dp", bit // seq)
    return lax.ppermute(block, axis, [(i, i ^ bit) for i in range(lax.axis_size(axis))])


def bits_of(count, unit=1):
    return [unit << k for k in range(count.bit_length() - 1)]


def gather(shard, order, me, shards):
    parts = {0: shard}
    for bit in order:
        for place in list(parts):
            parts[place | bit] = hop(parts[place], bit)
    table = jnp.zeros((shards, *shard.shape), shard.dtype)
    for place, part in parts.items():
        table = lax.dynamic_update_slice_in_dim(table, part[None], place ^ me, 0)
    return table


def total(terms):
    return sum(term.astype(F32) for term in terms)


def reduce_scatter(terms, order):
    for bit in order:
        half = terms[0].shape[0] // 2
        got = hop(total([term[half:] for term in terms]).astype(BF16), bit)
        terms = [term[:half] for term in terms] + [got]
    return total(terms)[0]


def slots_of(order, shards):
    return [
        sum(1 << (len(order) - 1 - k) for k, bit in enumerate(order) if place & bit)
        for place in range(shards)
    ]


def after(value, *earlier):
    return lax.optimization_barrier((value, *earlier))[0]


def on_device(tokens, out_grad, up_perm, down_perm, up_weight, down_weight):
    tok_rows, width = tokens.shape
    hid, _, size, _ = up_weight.shape
    groups, group = lax.axis_size("tensor"), lax.axis_index("tensor")
    away = groups // 2
    dp, seq = lax.axis_size("dp"), lax.axis_size("seq")
    shards = dp * seq
    me = lax.axis_index("dp") * seq + lax.axis_index("seq")
    seq_bits, dp_bits = bits_of(seq), bits_of(dp, seq)
    back = [(p, p + away) if p % 2 == 0 else (p + away, p) for p in range(away)]
    into = [(other, worker) for worker, other in back]
    works = (group % away % 2 == 0) != (group >= away)
    partner = (group + away) % groups

    rows = (tok_rows // 2, tok_rows - tok_rows // 2)
    lines = hid * 2 * size // shards

    def fetch(weight):
        shard = lax.dynamic_slice_in_dim(weight.reshape(-1, size), me * lines, lines, 0)
        return lax.ppermute(shard, "tensor", into)

    up_shard, down_shard = fetch(up_weight), fetch(down_weight)
    far = []
    for low, high in ((0, rows[0]), (rows[0], tok_rows)):
        pair = jnp.stack([tokens[low:high], out_grad[low:high]])
        far.append(lax.ppermute(pair, "tensor", into))
    up_far = gather(up_shard, dp_bits + seq_bits, me, shards).reshape(up_weight.shape)
    down_far = gather(down_shard, dp_bits[::-1] + seq_bits, me, shards).reshape(up_weight.shape)

    def block_ids(perm):
        flat = perm.reshape(2, -1)
        theirs = lax.dynamic_slice_in_dim(flat, partner * hid, hid, 1)
        mine = lax.dynamic_slice_in_dim(flat, group * hid, hid, 1)
        return jnp.concatenate([theirs[::-1], mine], axis=1)

    ids = jnp.concatenate(
        [block_ids(up_perm), block_ids(down_perm), jnp.full((1, 2 * hid), me, jnp.int32)]
    )

    orders = [dp_bits + seq_bits[1:], dp_bits[::-1] + seq_bits[1:]]
    slots = [slots_of(order, shards) for order in orders]
    each = min(4, hid)
    near = (tokens, out_grad)
    weights = (up_far, down_far, up_weight, down_weight)
    one = layer(True, rows, slots, each, ids, near, far[:1], *weights)
    first_out, far[1] = lax.optimization_barrier((one[2], far[1]))
    two = layer(False, rows, slots, each, ids, near, far, *weights, one[3:])

    got = [lax.ppermute(first_out, "tensor", back)]
    got[0], *two = lax.optimization_barrier((got[0], *two))
    got.append(lax.ppermute(two[2], "tensor", back))

    def plane_sum(keep, send):
        come = hop(send, seq_bits[0])
        return [reduce_scatter([keep[k], come[k]], orders[k]) for k in range(2)]

    theirs = [
        lax.ppermute(part.astype(BF16), "tensor", back) for part in plane_sum(two[3], two[4])
    ]
    mine = plane_sum(two[5], two[6])
    *got, mine[0] = lax.optimization_barrier((*got, mine[0]))

    def deliver(k):
        return jnp.concatenate(
            [jnp.where(works, part[k], come[k]) for part, come in zip((one, two), got)]
        )

    scale = float(tok_rows * shards) ** (-0.5)
    grads = [jnp.where(works, m, t.astype(F32)) * scale for m, t in zip(mine, theirs)]
    return deliver(0), deliver(1), grads[0], grads[1]


def solution(mesh):
    in_specs = (
        P(("dp", "seq"), "tensor"),
        P(("dp", "seq"), "tensor"),
        P(),
        P(),
        P("tensor", None, None, None),
        P("tensor", None, None, None),
    )
    out_specs = (
        P(("dp", "seq"), "tensor"),
        P(("dp", "seq"), "tensor"),
        P("tensor", None, ("dp", "seq"), None),
        P("tensor", None, ("dp", "seq"), None),
    )
    return jax.shard_map(
        on_device, mesh=mesh, in_specs=in_specs, out_specs=out_specs, check_vma=False
    )
```

```python
import functools
import math

import jax
import jax.numpy as jnp
from jax import lax
from jax.experimental import pallas as pl
from jax.experimental.pallas import tpu as pltpu
from jax.sharding import PartitionSpec as P

F32 = jnp.float32
BF16 = jnp.bfloat16
ROOT = math.sqrt(2.0 / math.pi)
CUBIC = 0.044715


def dot(a, b, over):
    return lax.dot_general(a, b, ((over[:1], over[1:]), ((), ())), preferred_element_type=F32)


def activate(pre, d_hidden):
    square = pre * pre
    tanh = jnp.tanh(pre * (ROOT + (ROOT * CUBIC) * square))
    cdf = 0.5 + 0.5 * tanh
    slope = cdf + pre * (0.5 - 0.5 * tanh * tanh) * (ROOT + (3.0 * ROOT * CUBIC) * square)
    return (pre * cdf).astype(BF16), (d_hidden * slope).astype(BF16)


def layer_kernel(last, slots, ids, *refs):
    refs = list(refs)
    take = lambda count: [refs.pop(0) for _ in range(count)]
    chunks = 2 if last else 1
    nears, fars = take(chunks), take(chunks)
    near, far = nears[-1], fars[-1]
    up, down = take(2)
    if last:
        hidden_kept, d_pre_kept, _ = take(3)
    (near_out,) = take(1)
    far_out = take(1 if last else 2)
    if last:
        sums = take(4)
    else:
        hidden_kept, d_pre_kept = take(2)
    out_acc, back_acc = take(2)
    if last:
        up_sum, down_sum = take(2)
    step = pl.program_id(0)
    steps = pl.num_programs(0)
    each, _, size, _ = up.shape

    @pl.when(step == 0)
    def _():
        out_acc[...] = jnp.zeros_like(out_acc)
        back_acc[...] = jnp.zeros_like(back_acc)

    theirs = step < steps // 2
    meets = theirs.astype(jnp.int32)

    def columns(block):
        return pl.ds(pl.multiple_of(block * size, size), size)

    def both(k, at, chunk=-1):
        return jnp.concatenate([nears[chunk][k, :, at[0]], fars[chunk][k, :, at[1]]], axis=1)

    def tall(first, second):
        return jnp.concatenate([first, second], axis=0)

    work = []
    for e in range(each):
        ins = [columns(ids[k, step * each + e]) for k in (0, 1)]
        outs = [columns(ids[k, step * each + e]) for k in (2, 3)]
        x_cat, g_cat = both(0, ins), both(1, outs)
        up_cat = jnp.concatenate([up[e, meets], up[e, 1 - meets]], axis=0)
        down_cat = jnp.concatenate([down[e, meets], down[e, 1 - meets]], axis=1)
        pre = dot(x_cat, up_cat, (1, 0))
        d_hidden = dot(g_cat, down_cat, (1, 1))
        work.append((ins, outs, x_cat, g_cat, up_cat, down_cat, pre, d_hidden))
    done = []
    for e, (ins, outs, x_cat, g_cat, up_cat, down_cat, pre, d_hidden) in enumerate(work):
        hidden, d_pre = activate(pre, d_hidden)
        done.append((dot(hidden, down_cat, (1, 0)), dot(d_pre, up_cat, (1, 1))))
        if last:
            up_sum[e] = dot(tall(both(0, ins, 0), x_cat), tall(d_pre_kept[e], d_pre), (0, 0))
            down_sum[e] = dot(tall(hidden_kept[e], hidden), tall(both(1, outs, 0), g_cat), (0, 0))
        else:
            hidden_kept[e] = hidden
            d_pre_kept[e] = d_pre
    for (ins, outs, *_), (out, back) in zip(work, done):
        for s in range(2):
            out_acc[s, :, outs[s]] += out[:, s * size : (s + 1) * size]
            back_acc[s, :, ins[s]] += back[:, s * size : (s + 1) * size]
    if last:
        me = ids[4, 0]
        shard = sums[0].shape[4]
        shards = size // shard

        def store(keep, send, flip):
            for e in range(each):
                for place in range(shards):
                    start = pl.multiple_of((place ^ me) * shard, shard)
                    to = send if place & 1 else keep
                    for s in range(2):
                        at = (1 - s if flip else s) * size
                        to[0, slots[0][place], e, s] = up_sum[
                            e, pl.ds(at + start, shard)
                        ].astype(BF16)
                        to[1, slots[1][place], e, s] = down_sum[
                            e, pl.ds(start, shard), at : at + size
                        ].astype(BF16)

        pl.when(theirs)(lambda: store(*sums[:2], True))
        pl.when(jnp.logical_not(theirs))(lambda: store(*sums[2:], False))

    @pl.when(step == steps - 1)
    def _():
        for k, acc in enumerate((out_acc, back_acc)):
            near_out[k] = acc[0].astype(BF16)
            row = 0
            for part in far_out:
                part[k] = acc[1, row : row + part.shape[1]].astype(BF16)
                row += part.shape[1]


def layer(slots, ids, nears, fars, weights, split=None, earlier=()):
    steps, _, size, _ = weights[0].shape
    hid = steps // 2
    _, count, width = nears[-1].shape
    shards = len(slots[0])
    last = split is None
    each = min(4, hid)
    turns = hid // each

    def whole(shape):
        return pl.BlockSpec(shape, lambda i, ids: (0,) * len(shape))

    def blocks(shape):
        return pl.BlockSpec((each, *shape[1:]), lambda i, ids: (i,) + (0,) * (len(shape) - 1))

    in_specs = [whole(part.shape) for part in (*nears, *fars)]
    in_specs += [blocks(weight.shape) for weight in weights]
    result = jax.ShapeDtypeStruct((2, count, width), BF16)
    out_shape = [result]
    out_specs = [whole(result.shape)]
    scratch = [pltpu.VMEM((2, count, width), F32)] * 2
    aliases = {}
    if last:
        in_specs += [blocks(part.shape) for part in earlier[:2]]
        in_specs += [pl.BlockSpec(memory_space=pl.ANY)]
        aliases = {len(in_specs): 1}
        out_shape.append(jax.ShapeDtypeStruct(earlier[2].shape, BF16))
        out_specs.append(whole(result.shape))
        shard = size // shards
        out_shape += [jax.ShapeDtypeStruct((2, shards // 2, hid, 2, shard, size), BF16)] * 4
        for part in range(2):
            out_specs += [
                pl.BlockSpec(
                    (2, shards // 2, each, 2, shard, size),
                    lambda i, ids, part=part: (
                        *(0, 0, jnp.clip(i - part * turns, 0, turns - 1)),
                        *(0, 0, 0),
                    ),
                )
            ] * 2
        scratch += [
            pltpu.VMEM((each, 2 * size, size), F32),
            pltpu.VMEM((each, size, 2 * size), F32),
        ]
    else:
        rest, behind = count - split[0], split[1]
        out_shape.append(jax.ShapeDtypeStruct((2, split[0], width), BF16))
        out_shape.append(jax.ShapeDtypeStruct((2, behind + rest, width), BF16))
        out_specs.append(whole((2, split[0], width)))
        out_specs.append(pl.BlockSpec((2, rest, width), lambda i, ids: (0, behind // rest, 0)))
        out_shape += [jax.ShapeDtypeStruct((steps, count, size), BF16)] * 2
        out_specs += [blocks(out_shape[-1].shape)] * 2
    return pl.pallas_call(
        functools.partial(layer_kernel, last, slots),
        out_shape=out_shape,
        grid_spec=pltpu.PrefetchScalarGridSpec(
            num_scalar_prefetch=1,
            grid=(2 * turns,),
            in_specs=in_specs,
            out_specs=out_specs,
            scratch_shapes=scratch,
        ),
        input_output_aliases=aliases,
        compiler_params=pltpu.CompilerParams(
            dimension_semantics=("arbitrary",), vmem_limit_bytes=60 << 20
        ),
        cost_estimate=pl.CostEstimate(flops=0, bytes_accessed=0, transcendentals=0),
    )(ids, *nears, *fars, *weights, *earlier)


def hop(block, bit):
    seq = lax.axis_size("seq")
    axis, bit = ("seq", bit) if bit < seq else ("dp", bit // seq)
    return lax.ppermute(block, axis, [(i, i ^ bit) for i in range(lax.axis_size(axis))])


def bits_of(count, unit=1):
    return [unit << k for k in range(count.bit_length() - 1)]


def gather(shard, order, me, weight):
    parts = {0: shard}
    for bit in order:
        for place in list(parts):
            parts[place | bit] = hop(parts[place], bit)
    ours = weight.reshape(-1, *shard.shape)
    table = jnp.concatenate([jnp.zeros_like(ours), ours])
    for place, part in parts.items():
        table = lax.dynamic_update_slice_in_dim(table, part[None], place ^ me, 0)
    return table.reshape(-1, *weight.shape[1:])


def total(terms):
    return sum(term.astype(F32) for term in terms)


def halve(terms, bit):
    half = terms[0].shape[0] // 2
    upper = total([term[half:] for term in terms]).astype(BF16)
    return [term[:half] for term in terms], upper, bit


def halved(terms, upper, bit):
    return [*terms, hop(upper, bit)]


def reduce_scatter(terms, order):
    for bit in order:
        terms = halved(*halve(terms, bit))
    return total(terms)[0]


def slots_of(order, shards):
    return [
        sum(1 << (len(order) - 1 - k) for k, bit in enumerate(order) if place & bit)
        for place in range(shards)
    ]


def after(value, *earlier):
    return lax.optimization_barrier((value, *earlier))[0]


def on_device(tokens, out_grad, up_perm, down_perm, up_weight, down_weight):
    tok_rows, width = tokens.shape
    hid, _, size, _ = up_weight.shape
    groups, group = lax.axis_size("tensor"), lax.axis_index("tensor")
    away = groups // 2
    dp, seq = lax.axis_size("dp"), lax.axis_size("seq")
    shards = dp * seq
    me = lax.axis_index("dp") * seq + lax.axis_index("seq")
    seq_bits, dp_bits = bits_of(seq), bits_of(dp, seq)
    back = [(p, p + away) if p % 2 == 0 else (p + away, p) for p in range(away)]
    into = [(other, worker) for worker, other in back]
    works = (group % away % 2 == 0) != (group >= away)
    partner = (group + away) % groups

    first, split = tok_rows // 2, 3 * tok_rows // 8
    lines = hid * 2 * size // shards

    def fetch(weight):
        shard = lax.dynamic_slice_in_dim(weight.reshape(-1, size), me * lines, lines, 0)
        return lax.ppermute(shard, "tensor", into)

    up_shard, down_shard = fetch(up_weight), fetch(down_weight)
    near = [
        jnp.stack([tokens[low:high], out_grad[low:high]])
        for low, high in ((0, first), (first, tok_rows))
    ]
    far = [lax.ppermute(near[0], "tensor", into)]
    far.append(lax.ppermute(near[1], "tensor", into))
    up = gather(up_shard, dp_bits + seq_bits, me, up_weight)
    down = gather(down_shard, dp_bits[::-1] + seq_bits, me, down_weight)
    weights = (up, down)

    def block_ids(perm):
        flat = perm.reshape(2, -1)
        theirs = lax.dynamic_slice_in_dim(flat, partner * hid, hid, 1)
        mine = lax.dynamic_slice_in_dim(flat, group * hid, hid, 1)
        return jnp.concatenate([theirs[::-1], mine], axis=1)

    ids = jnp.concatenate(
        [block_ids(up_perm), block_ids(down_perm), jnp.full((1, 2 * hid), me, jnp.int32)]
    )

    orders = [dp_bits + seq_bits[1:], dp_bits[::-1] + seq_bits[1:]]
    slots = [slots_of(order, shards) for order in orders]
    near_one, early, rest, *kept = layer(
        slots, ids, near[:1], far[:1], weights, (split, tok_rows - first)
    )
    early, far[1] = lax.optimization_barrier((early, far[1]))
    near_two, rest, *sums = layer(slots, ids, near, far, weights, earlier=(*kept, rest))
    early = lax.ppermute(early, "tensor", back)
    early, rest, near_two, sums = lax.optimization_barrier((early, rest, near_two, sums))
    rest = lax.ppermute(rest, "tensor", back)

    def terms_of(keep, send):
        come = hop(send, seq_bits[0])
        return [[keep[k], come[k]] for k in range(2)]

    theirs, mine = terms_of(*sums[:2]), terms_of(*sums[2:])
    theirs = [halved(*halve(theirs[k], orders[k][0])) for k in range(2)]
    mine = [halve(mine[k], orders[k][0]) for k in range(2)]
    uppers, theirs = lax.optimization_barrier(([upper for _, upper, _ in mine], theirs))
    mine = [halved(terms, upper, bit) for (terms, _, bit), upper in zip(mine, uppers)]
    theirs = [reduce_scatter(theirs[k], orders[k][1:]).astype(BF16) for k in range(2)]
    theirs, mine, rest = lax.optimization_barrier((theirs, mine, rest))
    theirs = [lax.ppermute(part, "tensor", back) for part in theirs]
    mine = [reduce_scatter(mine[k], orders[k][1:]) for k in range(2)]
    early, rest, mine[0] = lax.optimization_barrier((early, rest, mine[0]))

    def deliver(k):
        after = tok_rows - first
        ours = jnp.concatenate([near_one[k], near_two[k]])
        return jnp.where(works, ours, jnp.concatenate([early[k], rest[k, after:], rest[k, :after]]))

    scale = float(tok_rows * shards) ** (-0.5)
    grads = [jnp.where(works, m, t.astype(F32)) * scale for m, t in zip(mine, theirs)]
    return deliver(0), deliver(1), grads[0], grads[1]


def solution(mesh):
    in_specs = (
        P(("dp", "seq"), "tensor"),
        P(("dp", "seq"), "tensor"),
        P(),
        P(),
        P("tensor", None, None, None),
        P("tensor", None, None, None),
    )
    out_specs = (
        P(("dp", "seq"), "tensor"),
        P(("dp", "seq"), "tensor"),
        P("tensor", None, ("dp", "seq"), None),
        P("tensor", None, ("dp", "seq"), None),
    )
    return jax.shard_map(
        on_device, mesh=mesh, in_specs=in_specs, out_specs=out_specs, check_vma=False
    )
```

```python
import functools
import math

import jax
import jax.numpy as jnp
from jax import lax
from jax.experimental import pallas as pl
from jax.experimental.pallas import tpu as pltpu
from jax.sharding import PartitionSpec as P

F32 = jnp.float32
BF16 = jnp.bfloat16
ROOT = math.sqrt(2.0 / math.pi)
CUBIC = 0.044715


def dot(a, b, over):
    return lax.dot_general(a, b, ((over[:1], over[1:]), ((), ())), preferred_element_type=F32)


def activate(pre, d_hidden):
    square = pre * pre
    tanh = jnp.tanh(pre * (ROOT + (ROOT * CUBIC) * square))
    cdf = 0.5 + 0.5 * tanh
    slope = cdf + pre * (0.5 - 0.5 * tanh * tanh) * (ROOT + (3.0 * ROOT * CUBIC) * square)
    return (pre * cdf).astype(BF16), (d_hidden * slope).astype(BF16)


def layer_kernel(last, slots, ids, *refs):
    refs = list(refs)
    take = lambda count: [refs.pop(0) for _ in range(count)]
    chunks = 2 if last else 1
    nears, fars = take(chunks), take(chunks)
    near, far = nears[-1], fars[-1]
    weights = take(4)
    if last:
        hidden_kept, d_pre_kept = take(2)
    (near_out,) = take(1)
    far_out = take(1 if last else 2)
    if last:
        sums = take(4)
    else:
        hidden_kept, d_pre_kept = take(2)
    out_acc, back_acc = take(2)
    if last:
        up_sum, down_sum = take(2)
    step = pl.program_id(0)
    steps = pl.num_programs(0)
    each, _, size, _ = weights[0].shape

    @pl.when(step == 0)
    def _():
        out_acc[...] = jnp.zeros_like(out_acc)
        back_acc[...] = jnp.zeros_like(back_acc)

    theirs = step < steps // 2

    def columns(block):
        return pl.ds(pl.multiple_of(block * size, size), size)

    def both(k, at, chunk=-1):
        return jnp.concatenate([nears[chunk][k, :, at[0]], fars[chunk][k, :, at[1]]], axis=1)

    def tall(first, second):
        return jnp.concatenate([first, second], axis=0)

    def work_on(up, down, meets):
        work = []
        for e in range(each):
            ins = [columns(ids[k, step * each + e]) for k in (0, 1)]
            outs = [columns(ids[k, step * each + e]) for k in (2, 3)]
            x_cat, g_cat = both(0, ins), both(1, outs)
            up_cat = jnp.concatenate([up[e, meets], up[e, 1 - meets]], axis=0)
            down_cat = jnp.concatenate([down[e, meets], down[e, 1 - meets]], axis=1)
            pre = dot(x_cat, up_cat, (1, 0))
            d_hidden = dot(g_cat, down_cat, (1, 1))
            work.append((ins, outs, x_cat, g_cat, up_cat, down_cat, pre, d_hidden))
        done = []
        for e, (ins, outs, x_cat, g_cat, up_cat, down_cat, pre, d_hidden) in enumerate(work):
            hidden, d_pre = activate(pre, d_hidden)
            done.append((dot(hidden, down_cat, (1, 0)), dot(d_pre, up_cat, (1, 1))))
            if last:
                up_sum[e] = dot(tall(both(0, ins, 0), x_cat), tall(d_pre_kept[e], d_pre), (0, 0))
                down_sum[e] = dot(tall(hidden_kept[e], hidden), tall(both(1, outs, 0), g_cat), (0, 0))
            else:
                hidden_kept[e] = hidden
                d_pre_kept[e] = d_pre
        for (ins, outs, *_), (out, back) in zip(work, done):
            for s in range(2):
                out_acc[s, :, outs[s]] += out[:, s * size : (s + 1) * size]
                back_acc[s, :, ins[s]] += back[:, s * size : (s + 1) * size]

    pl.when(theirs)(lambda: work_on(*weights[:2], 1))
    pl.when(jnp.logical_not(theirs))(lambda: work_on(*weights[2:], 0))
    if last:
        me = ids[4, 0]
        shard = sums[0].shape[4]
        shards = size // shard

        def store(keep, send, flip):
            for e in range(each):
                for place in range(shards):
                    start = pl.multiple_of((place ^ me) * shard, shard)
                    to = send if place & 1 else keep
                    for s in range(2):
                        at = (1 - s if flip else s) * size
                        to[0, slots[0][place], e, s] = up_sum[
                            e, pl.ds(at + start, shard)
                        ].astype(BF16)
                        to[1, slots[1][place], e, s] = down_sum[
                            e, pl.ds(start, shard), at : at + size
                        ].astype(BF16)

        pl.when(theirs)(lambda: store(*sums[:2], True))
        pl.when(jnp.logical_not(theirs))(lambda: store(*sums[2:], False))

    @pl.when(step == steps - 1)
    def _():
        for k, acc in enumerate((out_acc, back_acc)):
            near_out[k] = acc[0].astype(BF16)
            row = 0
            for part in far_out:
                part[k] = acc[1, row : row + part.shape[1]].astype(BF16)
                row += part.shape[1]


def layer(slots, ids, nears, fars, weights, split=None, kept=()):
    hid, _, size, _ = weights[0].shape
    steps = 2 * hid
    _, count, width = nears[-1].shape
    shards = len(slots[0])
    last = split is None
    each = min(4, hid)
    turns = hid // each

    def whole(shape):
        return pl.BlockSpec(shape, lambda i, ids: (0,) * len(shape))

    def weight(part):
        return pl.BlockSpec(
            (each, 2, size, size),
            lambda i, ids: (jnp.clip(i - part * turns, 0, turns - 1), 0, 0, 0),
        )

    def blocks(shape):
        return pl.BlockSpec((each, *shape[1:]), lambda i, ids: (i,) + (0,) * (len(shape) - 1))

    in_specs = [whole(part.shape) for part in (*nears, *fars)]
    in_specs += [weight(part) for part in (0, 0, 1, 1)]
    result = jax.ShapeDtypeStruct((2, count, width), BF16)
    out_shape = [result]
    out_specs = [whole(result.shape)]
    scratch = [pltpu.VMEM((2, count, width), F32)] * 2
    if last:
        in_specs += [blocks(part.shape) for part in kept]
        out_shape.append(result)
        out_specs.append(whole(result.shape))
        shard = size // shards
        out_shape += [jax.ShapeDtypeStruct((2, shards // 2, hid, 2, shard, size), BF16)] * 4
        for part in range(2):
            out_specs += [
                pl.BlockSpec(
                    (2, shards // 2, each, 2, shard, size),
                    lambda i, ids, part=part: (
                        *(0, 0, jnp.clip(i - part * turns, 0, turns - 1)),
                        *(0, 0, 0),
                    ),
                )
            ] * 2
        scratch += [
            pltpu.VMEM((each, 2 * size, size), F32),
            pltpu.VMEM((each, size, 2 * size), F32),
        ]
    else:
        for part in (split, count - split):
            out_shape.append(jax.ShapeDtypeStruct((2, part, width), BF16))
            out_specs.append(whole((2, part, width)))
        out_shape += [jax.ShapeDtypeStruct((steps, count, size), BF16)] * 2
        out_specs += [blocks(out_shape[-1].shape)] * 2
    return pl.pallas_call(
        functools.partial(layer_kernel, last, slots),
        out_shape=out_shape,
        grid_spec=pltpu.PrefetchScalarGridSpec(
            num_scalar_prefetch=1,
            grid=(2 * turns,),
            in_specs=in_specs,
            out_specs=out_specs,
            scratch_shapes=scratch,
        ),
        compiler_params=pltpu.CompilerParams(
            dimension_semantics=("arbitrary",), vmem_limit_bytes=60 << 20
        ),
        cost_estimate=pl.CostEstimate(flops=0, bytes_accessed=0, transcendentals=0),
    )(ids, *nears, *fars, *weights, *kept)


def hop(block, bit):
    seq = lax.axis_size("seq")
    axis, bit = ("seq", bit) if bit < seq else ("dp", bit // seq)
    return lax.ppermute(block, axis, [(i, i ^ bit) for i in range(lax.axis_size(axis))])


def bits_of(count, unit=1):
    return [unit << k for k in range(count.bit_length() - 1)]


def gather(shard, order, me, shape):
    parts = {0: shard}
    for bit in order:
        for place in list(parts):
            parts[place | bit] = hop(parts[place], bit)
    table = jnp.zeros((len(parts), *shard.shape), shard.dtype)
    for place, part in parts.items():
        table = lax.dynamic_update_slice_in_dim(table, part[None], place ^ me, 0)
    return table.reshape(shape)


def total(terms):
    return sum(term.astype(F32) for term in terms)


def halve(terms, bit):
    half = terms[0].shape[0] // 2
    upper = total([term[half:] for term in terms]).astype(BF16)
    return [term[:half] for term in terms], upper, bit


def halved(terms, upper, bit):
    return [*terms, hop(upper, bit)]


def reduce_scatter(terms, order):
    for bit in order:
        terms = halved(*halve(terms, bit))
    return total(terms)[0]


def slots_of(order, shards):
    return [
        sum(1 << (len(order) - 1 - k) for k, bit in enumerate(order) if place & bit)
        for place in range(shards)
    ]


def after(value, *earlier):
    return lax.optimization_barrier((value, *earlier))[0]


def on_device(tokens, out_grad, up_perm, down_perm, up_weight, down_weight):
    tok_rows, width = tokens.shape
    hid, _, size, _ = up_weight.shape
    groups, group = lax.axis_size("tensor"), lax.axis_index("tensor")
    away = groups // 2
    dp, seq = lax.axis_size("dp"), lax.axis_size("seq")
    shards = dp * seq
    me = lax.axis_index("dp") * seq + lax.axis_index("seq")
    seq_bits, dp_bits = bits_of(seq), bits_of(dp, seq)
    back = [(p, p + away) if p % 2 == 0 else (p + away, p) for p in range(away)]
    into = [(other, worker) for worker, other in back]
    works = (group % away % 2 == 0) != (group >= away)
    partner = (group + away) % groups

    first, split = 11 * tok_rows // 16, 3 * tok_rows // 8
    lines = hid * 2 * size // shards

    def fetch(weight):
        shard = lax.dynamic_slice_in_dim(weight.reshape(-1, size), me * lines, lines, 0)
        return lax.ppermute(shard, "tensor", into)

    up_shard, down_shard = fetch(up_weight), fetch(down_weight)
    near = [
        jnp.stack([tokens[low:high], out_grad[low:high]])
        for low, high in ((0, first), (first, tok_rows))
    ]
    far = [lax.ppermute(near[0], "tensor", into)]
    later, up_shard = lax.optimization_barrier((near[1], up_shard))
    far.append(lax.ppermute(later, "tensor", into))
    up = gather(up_shard, dp_bits + seq_bits, me, up_weight.shape)
    down = gather(down_shard, dp_bits[::-1] + seq_bits, me, up_weight.shape)
    weights = (up, down, up_weight, down_weight)

    def block_ids(perm):
        flat = perm.reshape(2, -1)
        theirs = lax.dynamic_slice_in_dim(flat, partner * hid, hid, 1)
        mine = lax.dynamic_slice_in_dim(flat, group * hid, hid, 1)
        return jnp.concatenate([theirs[::-1], mine], axis=1)

    ids = jnp.concatenate(
        [block_ids(up_perm), block_ids(down_perm), jnp.full((1, 2 * hid), me, jnp.int32)]
    )

    orders = [dp_bits + seq_bits[1:], dp_bits[::-1] + seq_bits[1:]]
    slots = [slots_of(order, shards) for order in orders]
    near_one, early, middle, *kept = layer(slots, ids, near[:1], far[:1], weights, split)
    early, middle, far[1] = lax.optimization_barrier((early, middle, far[1]))
    near_two, late, *sums = layer(slots, ids, near, far, weights, kept=kept)
    early = lax.ppermute(early, "tensor", back)
    early, near_two, late, sums = lax.optimization_barrier((early, near_two, late, sums))
    middle = lax.ppermute(middle, "tensor", back)
    late = lax.ppermute(late, "tensor", back)

    def terms_of(keep, send):
        come = hop(send, seq_bits[0])
        return [[keep[k], come[k]] for k in range(2)]

    theirs, mine = terms_of(*sums[:2]), terms_of(*sums[2:])
    theirs = [halved(*halve(theirs[k], orders[k][0])) for k in range(2)]
    mine = [halve(mine[k], orders[k][0]) for k in range(2)]
    uppers, theirs, middle = lax.optimization_barrier(
        ([upper for _, upper, _ in mine], theirs, middle)
    )
    mine = [halved(terms, upper, bit) for (terms, _, bit), upper in zip(mine, uppers)]
    theirs = [reduce_scatter(theirs[k], orders[k][1:]).astype(BF16) for k in range(2)]
    theirs = [lax.ppermute(part, "tensor", back) for part in theirs]
    theirs[1], mine, late = lax.optimization_barrier((theirs[1], mine, late))
    mine = [reduce_scatter(mine[k], orders[k][1:]) for k in range(2)]

    def deliver(k):
        ours = jnp.concatenate([near_one[k], near_two[k]])
        return jnp.where(works, ours, jnp.concatenate([early[k], middle[k], late[k]]))

    scale = float(tok_rows * shards) ** (-0.5)
    grads = [jnp.where(works, m, t.astype(F32)) * scale for m, t in zip(mine, theirs)]
    return deliver(0), deliver(1), grads[0], grads[1]


def solution(mesh):
    in_specs = (
        P(("dp", "seq"), "tensor"),
        P(("dp", "seq"), "tensor"),
        P(),
        P(),
        P("tensor", None, None, None),
        P("tensor", None, None, None),
    )
    out_specs = (
        P(("dp", "seq"), "tensor"),
        P(("dp", "seq"), "tensor"),
        P("tensor", None, ("dp", "seq"), None),
        P("tensor", None, ("dp", "seq"), None),
    )
    return jax.shard_map(
        on_device, mesh=mesh, in_specs=in_specs, out_specs=out_specs, check_vma=False
    )
```

```python
import functools
import math

import jax
import jax.numpy as jnp
from jax import lax
from jax.experimental import pallas as pl
from jax.experimental.pallas import tpu as pltpu
from jax.sharding import PartitionSpec as P

F32 = jnp.float32
BF16 = jnp.bfloat16
ROOT = math.sqrt(2.0 / math.pi)
CUBIC = 0.044715


def dot(a, b, over):
    return lax.dot_general(a, b, ((over[:1], over[1:]), ((), ())), preferred_element_type=F32)


def activate(pre, d_hidden):
    square = pre * pre
    tanh = jnp.tanh(pre * (ROOT + (ROOT * CUBIC) * square))
    cdf = 0.5 + 0.5 * tanh
    slope = cdf + pre * (0.5 - 0.5 * tanh * tanh) * (ROOT + (3.0 * ROOT * CUBIC) * square)
    return (pre * cdf).astype(BF16), (d_hidden * slope).astype(BF16)


def layer_kernel(last, slots, ids, *refs):
    refs = list(refs)
    take = lambda count: [refs.pop(0) for _ in range(count)]
    chunks = 2 if last else 1
    nears, fars = take(chunks), take(chunks)
    near, far = nears[-1], fars[-1]
    weights = take(4)
    if last:
        hidden_kept, d_pre_kept = take(2)
    (near_out,) = take(1)
    far_out = take(1 if last else 2)
    if last:
        sums = take(4)
    else:
        hidden_kept, d_pre_kept = take(2)
    out_acc, back_acc = take(2)
    if last:
        up_sum, down_sum = take(2)
    step = pl.program_id(0)
    steps = pl.num_programs(0)
    each, _, size, _ = weights[0].shape

    @pl.when(step == 0)
    def _():
        out_acc[...] = jnp.zeros_like(out_acc)
        back_acc[...] = jnp.zeros_like(back_acc)

    theirs = step < steps // 2

    def columns(block):
        return pl.ds(pl.multiple_of(block * size, size), size)

    def both(k, at, chunk=-1):
        return jnp.concatenate([nears[chunk][k, :, at[0]], fars[chunk][k, :, at[1]]], axis=1)

    def tall(first, second):
        return jnp.concatenate([first, second], axis=0)

    def work_on(up, down, meets):
        work = []
        for e in range(each):
            ins = [columns(ids[k, step * each + e]) for k in (0, 1)]
            outs = [columns(ids[k, step * each + e]) for k in (2, 3)]
            x_cat, g_cat = both(0, ins), both(1, outs)
            up_cat = jnp.concatenate([up[e, meets], up[e, 1 - meets]], axis=0)
            down_cat = jnp.concatenate([down[e, meets], down[e, 1 - meets]], axis=1)
            pre = dot(x_cat, up_cat, (1, 0))
            d_hidden = dot(g_cat, down_cat, (1, 1))
            work.append((ins, outs, x_cat, g_cat, up_cat, down_cat, pre, d_hidden))
        done = []
        for e, (ins, outs, x_cat, g_cat, up_cat, down_cat, pre, d_hidden) in enumerate(work):
            hidden, d_pre = activate(pre, d_hidden)
            done.append((dot(hidden, down_cat, (1, 0)), dot(d_pre, up_cat, (1, 1))))
            if last:
                up_sum[e] = dot(tall(both(0, ins, 0), x_cat), tall(d_pre_kept[e], d_pre), (0, 0))
                down_sum[e] = dot(tall(hidden_kept[e], hidden), tall(both(1, outs, 0), g_cat), (0, 0))
            else:
                hidden_kept[e] = hidden
                d_pre_kept[e] = d_pre
        for (ins, outs, *_), (out, back) in zip(work, done):
            for s in range(2):
                out_acc[s, :, outs[s]] += out[:, s * size : (s + 1) * size]
                back_acc[s, :, ins[s]] += back[:, s * size : (s + 1) * size]

    works = ids[5, 0] != 0
    pl.when(works & theirs)(lambda: work_on(*weights[:2], 1))
    pl.when(works & jnp.logical_not(theirs))(lambda: work_on(*weights[2:], 0))
    if last:
        me = ids[4, 0]
        shard = sums[0].shape[4]
        shards = size // shard

        def store(keep, send, flip):
            for e in range(each):
                for place in range(shards):
                    start = pl.multiple_of((place ^ me) * shard, shard)
                    to = send if place & 1 else keep
                    for s in range(2):
                        at = (1 - s if flip else s) * size
                        to[0, slots[0][place], e, s] = up_sum[
                            e, pl.ds(at + start, shard)
                        ].astype(BF16)
                        to[1, slots[1][place], e, s] = down_sum[
                            e, pl.ds(start, shard), at : at + size
                        ].astype(BF16)

        pl.when(works & theirs)(lambda: store(*sums[:2], True))
        pl.when(works & jnp.logical_not(theirs))(lambda: store(*sums[2:], False))

    @pl.when(step == steps - 1)
    def _():
        for k, acc in enumerate((out_acc, back_acc)):
            near_out[k] = acc[0].astype(BF16)
            row = 0
            for part in far_out:
                part[k] = acc[1, row : row + part.shape[1]].astype(BF16)
                row += part.shape[1]


def layer(slots, ids, nears, fars, weights, split=None, kept=()):
    hid, _, size, _ = weights[0].shape
    steps = 2 * hid
    _, count, width = nears[-1].shape
    shards = len(slots[0])
    last = split is None
    each = min(4, hid)
    turns = hid // each

    def whole(shape):
        return pl.BlockSpec(shape, lambda i, ids: (0,) * len(shape))

    def weight(part):
        return pl.BlockSpec(
            (each, 2, size, size),
            lambda i, ids: (jnp.clip(i - part * turns, 0, turns - 1), 0, 0, 0),
        )

    def blocks(shape):
        return pl.BlockSpec((each, *shape[1:]), lambda i, ids: (i,) + (0,) * (len(shape) - 1))

    in_specs = [whole(part.shape) for part in (*nears, *fars)]
    in_specs += [weight(part) for part in (0, 0, 1, 1)]
    result = jax.ShapeDtypeStruct((2, count, width), BF16)
    out_shape = [result]
    out_specs = [whole(result.shape)]
    scratch = [pltpu.VMEM((2, count, width), F32)] * 2
    if last:
        in_specs += [blocks(part.shape) for part in kept]
        out_shape.append(result)
        out_specs.append(whole(result.shape))
        shard = size // shards
        out_shape += [jax.ShapeDtypeStruct((2, shards // 2, hid, 2, shard, size), BF16)] * 4
        for part in range(2):
            out_specs += [
                pl.BlockSpec(
                    (2, shards // 2, each, 2, shard, size),
                    lambda i, ids, part=part: (
                        *(0, 0, jnp.clip(i - part * turns, 0, turns - 1)),
                        *(0, 0, 0),
                    ),
                )
            ] * 2
        scratch += [
            pltpu.VMEM((each, 2 * size, size), F32),
            pltpu.VMEM((each, size, 2 * size), F32),
        ]
    else:
        for part in (split, count - split):
            out_shape.append(jax.ShapeDtypeStruct((2, part, width), BF16))
            out_specs.append(whole((2, part, width)))
        out_shape += [jax.ShapeDtypeStruct((steps, count, size), BF16)] * 2
        out_specs += [blocks(out_shape[-1].shape)] * 2
    return pl.pallas_call(
        functools.partial(layer_kernel, last, slots),
        out_shape=out_shape,
        grid_spec=pltpu.PrefetchScalarGridSpec(
            num_scalar_prefetch=1,
            grid=(2 * turns,),
            in_specs=in_specs,
            out_specs=out_specs,
            scratch_shapes=scratch,
        ),
        compiler_params=pltpu.CompilerParams(
            dimension_semantics=("arbitrary",), vmem_limit_bytes=60 << 20
        ),
        cost_estimate=pl.CostEstimate(flops=0, bytes_accessed=0, transcendentals=0),
    )(ids, *nears, *fars, *weights, *kept)


def hop(block, bit):
    seq = lax.axis_size("seq")
    axis, bit = ("seq", bit) if bit < seq else ("dp", bit // seq)
    return lax.ppermute(block, axis, [(i, i ^ bit) for i in range(lax.axis_size(axis))])


def bits_of(count, unit=1):
    return [unit << k for k in range(count.bit_length() - 1)]


def gather(shard, order, me, shape):
    parts = {0: shard}
    for bit in order:
        for place in list(parts):
            parts[place | bit] = hop(parts[place], bit)
    table = jnp.zeros((len(parts), *shard.shape), shard.dtype)
    for place, part in parts.items():
        table = lax.dynamic_update_slice_in_dim(table, part[None], place ^ me, 0)
    return table.reshape(shape)


def total(terms):
    return sum(term.astype(F32) for term in terms)


def halve(terms, bit):
    half = terms[0].shape[0] // 2
    upper = total([term[half:] for term in terms]).astype(BF16)
    return [term[:half] for term in terms], upper, bit


def halved(terms, upper, bit):
    return [*terms, hop(upper, bit)]


def reduce_scatter(terms, order):
    for bit in order:
        terms = halved(*halve(terms, bit))
    return total(terms)[0]


def slots_of(order, shards):
    return [
        sum(1 << (len(order) - 1 - k) for k, bit in enumerate(order) if place & bit)
        for place in range(shards)
    ]


def after(value, *earlier):
    return lax.optimization_barrier((value, *earlier))[0]


def on_device(tokens, out_grad, up_perm, down_perm, up_weight, down_weight):
    tok_rows, width = tokens.shape
    hid, _, size, _ = up_weight.shape
    groups, group = lax.axis_size("tensor"), lax.axis_index("tensor")
    away = groups // 2
    dp, seq = lax.axis_size("dp"), lax.axis_size("seq")
    shards = dp * seq
    me = lax.axis_index("dp") * seq + lax.axis_index("seq")
    seq_bits, dp_bits = bits_of(seq), bits_of(dp, seq)
    back = [(p, p + away) if p % 2 == 0 else (p + away, p) for p in range(away)]
    into = [(other, worker) for worker, other in back]
    works = (group % away % 2 == 0) != (group >= away)
    partner = (group + away) % groups

    first, split = 21 * tok_rows // 32, 12 * tok_rows // 32
    lines = hid * 2 * size // shards

    def fetch(weight):
        shard = lax.dynamic_slice_in_dim(weight.reshape(-1, size), me * lines, lines, 0)
        return lax.ppermute(shard, "tensor", into)

    up_shard, down_shard = fetch(up_weight), fetch(down_weight)
    near = [
        jnp.stack([tokens[low:high], out_grad[low:high]])
        for low, high in ((0, first), (first, tok_rows))
    ]
    far = [lax.ppermute(near[0], "tensor", into)]
    later, up_shard = lax.optimization_barrier((near[1], up_shard))
    far.append(lax.ppermute(later, "tensor", into))
    up = gather(up_shard, dp_bits + seq_bits, me, up_weight.shape)
    down = gather(down_shard, dp_bits[::-1] + seq_bits, me, up_weight.shape)
    weights = (up, down, up_weight, down_weight)

    def block_ids(perm):
        flat = perm.reshape(2, -1)
        theirs = lax.dynamic_slice_in_dim(flat, partner * hid, hid, 1)
        mine = lax.dynamic_slice_in_dim(flat, group * hid, hid, 1)
        return jnp.concatenate([theirs[::-1], mine], axis=1)

    flags = [jnp.full((1, 2 * hid), flag, jnp.int32) for flag in (me, works)]
    ids = jnp.concatenate([block_ids(up_perm), block_ids(down_perm), *flags])

    orders = [dp_bits + seq_bits[1:], dp_bits[::-1] + seq_bits[1:]]
    slots = [slots_of(order, shards) for order in orders]
    near_one, early, middle, *kept = layer(slots, ids, near[:1], far[:1], weights, split)
    early, middle, far[1] = lax.optimization_barrier((early, middle, far[1]))
    near_two, late, *sums = layer(slots, ids, near, far, weights, kept=kept)
    early = lax.ppermute(early, "tensor", back)
    early, near_two, late, sums = lax.optimization_barrier((early, near_two, late, sums))
    middle = lax.ppermute(middle, "tensor", back)
    late = lax.ppermute(late, "tensor", back)

    def terms_of(keep, send):
        come = hop(send, seq_bits[0])
        return [[keep[k], come[k]] for k in range(2)]

    theirs, mine = terms_of(*sums[:2]), terms_of(*sums[2:])
    theirs = [halved(*halve(theirs[k], orders[k][0])) for k in range(2)]
    mine = [halve(mine[k], orders[k][0]) for k in range(2)]
    uppers, theirs, middle = lax.optimization_barrier(
        ([upper for _, upper, _ in mine], theirs, middle)
    )
    mine = [halved(terms, upper, bit) for (terms, _, bit), upper in zip(mine, uppers)]
    theirs = [reduce_scatter(theirs[k], orders[k][1:]).astype(BF16) for k in range(2)]
    theirs = [lax.ppermute(part, "tensor", back) for part in theirs]
    theirs[1], mine, late = lax.optimization_barrier((theirs[1], mine, late))
    mine = [reduce_scatter(mine[k], orders[k][1:]) for k in range(2)]

    def deliver(k):
        ours = jnp.concatenate([near_one[k], near_two[k]])
        return jnp.where(works, ours, jnp.concatenate([early[k], middle[k], late[k]]))

    scale = float(tok_rows * shards) ** (-0.5)
    grads = [jnp.where(works, m, t.astype(F32)) * scale for m, t in zip(mine, theirs)]
    return deliver(0), deliver(1), grads[0], grads[1]


def solution(mesh):
    in_specs = (
        P(("dp", "seq"), "tensor"),
        P(("dp", "seq"), "tensor"),
        P(),
        P(),
        P("tensor", None, None, None),
        P("tensor", None, None, None),
    )
    out_specs = (
        P(("dp", "seq"), "tensor"),
        P(("dp", "seq"), "tensor"),
        P("tensor", None, ("dp", "seq"), None),
        P("tensor", None, ("dp", "seq"), None),
    )
    return jax.shard_map(
        on_device, mesh=mesh, in_specs=in_specs, out_specs=out_specs, check_vma=False
    )
```

```python
import functools
import math

import jax
import jax.numpy as jnp
from jax import lax
from jax.experimental import pallas as pl
from jax.experimental.pallas import tpu as pltpu
from jax.sharding import PartitionSpec as P

F32 = jnp.float32
BF16 = jnp.bfloat16
ROOT = math.sqrt(2.0 / math.pi)
CUBIC = 0.044715


def dot(a, b, over):
    return lax.dot_general(a, b, ((over[:1], over[1:]), ((), ())), preferred_element_type=F32)


def activate(pre, d_hidden):
    square = pre * pre
    tanh = jnp.tanh(pre * (ROOT + (ROOT * CUBIC) * square))
    cdf = 0.5 + 0.5 * tanh
    slope = cdf + pre * (0.5 - 0.5 * tanh * tanh) * (ROOT + (3.0 * ROOT * CUBIC) * square)
    return (pre * cdf).astype(BF16), (d_hidden * slope).astype(BF16)


def layer_kernel(last, slots, ids, *refs):
    refs = list(refs)
    take = lambda count: [refs.pop(0) for _ in range(count)]
    chunks = 2 if last else 1
    nears, fars = take(chunks), take(chunks)
    near, far = nears[-1], fars[-1]
    weights = take(4)
    if last:
        hidden_kept, d_pre_kept = take(2)
    (near_out,) = take(1)
    far_out = take(1 if last else 2)
    if last:
        sums = take(4)
    else:
        hidden_kept, d_pre_kept = take(2)
    out_acc, back_acc = take(2)
    if last:
        up_sum, down_sum = take(2)
    step = pl.program_id(0)
    steps = pl.num_programs(0)
    each, _, size, _ = weights[0].shape

    works = ids[5, 0] != 0

    @pl.when(works & (step == 0))
    def _():
        out_acc[...] = jnp.zeros_like(out_acc)
        back_acc[...] = jnp.zeros_like(back_acc)

    theirs = step < steps // 2

    def columns(block):
        return pl.ds(pl.multiple_of(block * size, size), size)

    def both(k, at, chunk=-1):
        return jnp.concatenate([nears[chunk][k, :, at[0]], fars[chunk][k, :, at[1]]], axis=1)

    def tall(first, second):
        return jnp.concatenate([first, second], axis=0)

    def work_on(up, down, meets):
        work = []
        for e in range(each):
            ins = [columns(ids[k, step * each + e]) for k in (0, 1)]
            outs = [columns(ids[k, step * each + e]) for k in (2, 3)]
            x_cat, g_cat = both(0, ins), both(1, outs)
            up_cat = jnp.concatenate([up[e, meets], up[e, 1 - meets]], axis=0)
            down_cat = jnp.concatenate([down[e, meets], down[e, 1 - meets]], axis=1)
            pre = dot(x_cat, up_cat, (1, 0))
            d_hidden = dot(g_cat, down_cat, (1, 1))
            work.append((ins, outs, x_cat, g_cat, up_cat, down_cat, pre, d_hidden))
        done = []
        for e, (ins, outs, x_cat, g_cat, up_cat, down_cat, pre, d_hidden) in enumerate(work):
            hidden, d_pre = activate(pre, d_hidden)
            done.append((dot(hidden, down_cat, (1, 0)), dot(d_pre, up_cat, (1, 1))))
            if last:
                up_sum[e] = dot(tall(both(0, ins, 0), x_cat), tall(d_pre_kept[e], d_pre), (0, 0))
                down_sum[e] = dot(tall(hidden_kept[e], hidden), tall(both(1, outs, 0), g_cat), (0, 0))
            else:
                hidden_kept[e] = hidden
                d_pre_kept[e] = d_pre
        for (ins, outs, *_), (out, back) in zip(work, done):
            for s in range(2):
                out_acc[s, :, outs[s]] += out[:, s * size : (s + 1) * size]
                back_acc[s, :, ins[s]] += back[:, s * size : (s + 1) * size]

    pl.when(works & theirs)(lambda: work_on(*weights[:2], 1))
    pl.when(works & jnp.logical_not(theirs))(lambda: work_on(*weights[2:], 0))
    if last:
        me = ids[4, 0]
        shard = sums[0].shape[4]
        shards = size // shard

        def store(keep, send, flip):
            for e in range(each):
                for place in range(shards):
                    start = pl.multiple_of((place ^ me) * shard, shard)
                    to = send if place & 1 else keep
                    for s in range(2):
                        at = (1 - s if flip else s) * size
                        to[0, slots[0][place], e, s] = up_sum[
                            e, pl.ds(at + start, shard)
                        ].astype(BF16)
                        to[1, slots[1][place], e, s] = down_sum[
                            e, pl.ds(start, shard), at : at + size
                        ].astype(BF16)

        pl.when(works & theirs)(lambda: store(*sums[:2], True))
        pl.when(works & jnp.logical_not(theirs))(lambda: store(*sums[2:], False))

    @pl.when(works & (step == steps - 1))
    def _():
        for k, acc in enumerate((out_acc, back_acc)):
            near_out[k] = acc[0].astype(BF16)
            row = 0
            for part in far_out:
                part[k] = acc[1, row : row + part.shape[1]].astype(BF16)
                row += part.shape[1]


def layer(slots, ids, nears, fars, weights, split=None, kept=()):
    hid, _, size, _ = weights[0].shape
    steps = 2 * hid
    _, count, width = nears[-1].shape
    shards = len(slots[0])
    last = split is None
    each = min(4, hid)
    turns = hid // each

    def whole(shape):
        return pl.BlockSpec(shape, lambda i, ids: (0,) * len(shape))

    def weight(part):
        return pl.BlockSpec(
            (each, 2, size, size),
            lambda i, ids: (jnp.clip(i - part * turns, 0, turns - 1) * ids[5, 0], 0, 0, 0),
        )

    def blocks(shape):
        return pl.BlockSpec((each, *shape[1:]), lambda i, ids: (i,) + (0,) * (len(shape) - 1))

    in_specs = [whole(part.shape) for part in (*nears, *fars)]
    in_specs += [weight(part) for part in (0, 0, 1, 1)]
    result = jax.ShapeDtypeStruct((2, count, width), BF16)
    out_shape = [result]
    out_specs = [whole(result.shape)]
    scratch = [pltpu.VMEM((2, count, width), F32)] * 2
    if last:
        in_specs += [blocks(part.shape) for part in kept]
        out_shape.append(result)
        out_specs.append(whole(result.shape))
        shard = size // shards
        out_shape += [jax.ShapeDtypeStruct((2, shards // 2, hid, 2, shard, size), BF16)] * 4
        for part in range(2):
            out_specs += [
                pl.BlockSpec(
                    (2, shards // 2, each, 2, shard, size),
                    lambda i, ids, part=part: (
                        *(0, 0, jnp.clip(i - part * turns, 0, turns - 1)),
                        *(0, 0, 0),
                    ),
                )
            ] * 2
        scratch += [
            pltpu.VMEM((each, 2 * size, size), F32),
            pltpu.VMEM((each, size, 2 * size), F32),
        ]
    else:
        for part in (split, count - split):
            out_shape.append(jax.ShapeDtypeStruct((2, part, width), BF16))
            out_specs.append(whole((2, part, width)))
        out_shape += [jax.ShapeDtypeStruct((steps, count, size), BF16)] * 2
        out_specs += [blocks(out_shape[-1].shape)] * 2
    return pl.pallas_call(
        functools.partial(layer_kernel, last, slots),
        out_shape=out_shape,
        grid_spec=pltpu.PrefetchScalarGridSpec(
            num_scalar_prefetch=1,
            grid=(2 * turns,),
            in_specs=in_specs,
            out_specs=out_specs,
            scratch_shapes=scratch,
        ),
        compiler_params=pltpu.CompilerParams(
            dimension_semantics=("arbitrary",), vmem_limit_bytes=60 << 20
        ),
        cost_estimate=pl.CostEstimate(flops=0, bytes_accessed=0, transcendentals=0),
    )(ids, *nears, *fars, *weights, *kept)


def hop(block, bit):
    seq = lax.axis_size("seq")
    axis, bit = ("seq", bit) if bit < seq else ("dp", bit // seq)
    return lax.ppermute(block, axis, [(i, i ^ bit) for i in range(lax.axis_size(axis))])


def bits_of(count, unit=1):
    return [unit << k for k in range(count.bit_length() - 1)]


def gather(shard, order, me, shape):
    parts = {0: shard}
    for bit in order:
        for place in list(parts):
            parts[place | bit] = hop(parts[place], bit)
    table = jnp.zeros((len(parts), *shard.shape), shard.dtype)
    for place, part in parts.items():
        table = lax.dynamic_update_slice_in_dim(table, part[None], place ^ me, 0)
    return table.reshape(shape)


def total(terms):
    return sum(term.astype(F32) for term in terms)


def halve(terms, bit):
    half = terms[0].shape[0] // 2
    upper = total([term[half:] for term in terms]).astype(BF16)
    return [term[:half] for term in terms], upper, bit


def halved(terms, upper, bit):
    return [*terms, hop(upper, bit)]


def reduce_scatter(terms, order):
    for bit in order:
        terms = halved(*halve(terms, bit))
    return total(terms)[0]


def slots_of(order, shards):
    return [
        sum(1 << (len(order) - 1 - k) for k, bit in enumerate(order) if place & bit)
        for place in range(shards)
    ]


def after(value, *earlier):
    return lax.optimization_barrier((value, *earlier))[0]


def on_device(tokens, out_grad, up_perm, down_perm, up_weight, down_weight):
    tok_rows, width = tokens.shape
    hid, _, size, _ = up_weight.shape
    groups, group = lax.axis_size("tensor"), lax.axis_index("tensor")
    away = groups // 2
    dp, seq = lax.axis_size("dp"), lax.axis_size("seq")
    shards = dp * seq
    me = lax.axis_index("dp") * seq + lax.axis_index("seq")
    seq_bits, dp_bits = bits_of(seq), bits_of(dp, seq)
    back = [(p, p + away) if p % 2 == 0 else (p + away, p) for p in range(away)]
    into = [(other, worker) for worker, other in back]
    works = (group % away % 2 == 0) != (group >= away)
    partner = (group + away) % groups

    first, split = 21 * tok_rows // 32, 11 * tok_rows // 32
    lines = hid * 2 * size // shards

    def fetch(weight):
        shard = lax.dynamic_slice_in_dim(weight.reshape(-1, size), me * lines, lines, 0)
        return lax.ppermute(shard, "tensor", into)

    up_shard, down_shard = fetch(up_weight), fetch(down_weight)
    near = [
        jnp.stack([tokens[low:high], out_grad[low:high]])
        for low, high in ((0, first), (first, tok_rows))
    ]
    far = [lax.ppermute(near[0], "tensor", into)]
    later, up_shard = lax.optimization_barrier((near[1], up_shard))
    far.append(lax.ppermute(later, "tensor", into))
    up = gather(up_shard, dp_bits + seq_bits, me, up_weight.shape)
    down = gather(down_shard, dp_bits[::-1] + seq_bits, me, up_weight.shape)
    weights = (up, down, up_weight, down_weight)

    def block_ids(perm):
        flat = perm.reshape(2, -1)
        theirs = lax.dynamic_slice_in_dim(flat, partner * hid, hid, 1)
        mine = lax.dynamic_slice_in_dim(flat, group * hid, hid, 1)
        return jnp.concatenate([theirs[::-1], mine], axis=1)

    flags = [jnp.full((1, 2 * hid), flag, jnp.int32) for flag in (me, works)]
    ids = jnp.concatenate([block_ids(up_perm), block_ids(down_perm), *flags])

    orders = [dp_bits + seq_bits[1:], dp_bits[::-1] + seq_bits[1:]]
    slots = [slots_of(order, shards) for order in orders]
    near_one, early, middle, *kept = layer(slots, ids, near[:1], far[:1], weights, split)
    early, middle, far[1] = lax.optimization_barrier((early, middle, far[1]))
    near_two, late, *sums = layer(slots, ids, near, far, weights, kept=kept)
    early = lax.ppermute(early, "tensor", back)
    early, near_two, late, sums = lax.optimization_barrier((early, near_two, late, sums))
    middle = lax.ppermute(middle, "tensor", back)
    late = lax.ppermute(late, "tensor", back)

    def terms_of(keep, send):
        come = hop(send, seq_bits[0])
        return [[keep[k], come[k]] for k in range(2)]

    theirs, mine = terms_of(*sums[:2]), terms_of(*sums[2:])
    theirs = [halved(*halve(theirs[k], orders[k][0])) for k in range(2)]
    mine = [halve(mine[k], orders[k][0]) for k in range(2)]
    uppers, theirs, middle = lax.optimization_barrier(
        ([upper for _, upper, _ in mine], theirs, middle)
    )
    mine = [halved(terms, upper, bit) for (terms, _, bit), upper in zip(mine, uppers)]
    theirs = [reduce_scatter(theirs[k], orders[k][1:]).astype(BF16) for k in range(2)]
    theirs = [lax.ppermute(part, "tensor", back) for part in theirs]
    theirs[1], mine, late = lax.optimization_barrier((theirs[1], mine, late))
    mine = [reduce_scatter(mine[k], orders[k][1:]) for k in range(2)]

    def deliver(k):
        ours = jnp.concatenate([near_one[k], near_two[k]])
        return jnp.where(works, ours, jnp.concatenate([early[k], middle[k], late[k]]))

    scale = float(tok_rows * shards) ** (-0.5)
    grads = [jnp.where(works, m, t.astype(F32)) * scale for m, t in zip(mine, theirs)]
    return deliver(0), deliver(1), grads[0], grads[1]


def solution(mesh):
    in_specs = (
        P(("dp", "seq"), "tensor"),
        P(("dp", "seq"), "tensor"),
        P(),
        P(),
        P("tensor", None, None, None),
        P("tensor", None, None, None),
    )
    out_specs = (
        P(("dp", "seq"), "tensor"),
        P(("dp", "seq"), "tensor"),
        P("tensor", None, ("dp", "seq"), None),
        P("tensor", None, ("dp", "seq"), None),
    )
    return jax.shard_map(
        on_device, mesh=mesh, in_specs=in_specs, out_specs=out_specs, check_vma=False
    )
```
